128 devices in a mesh: dp: 16 (over y, z_lo, core), tensor: 8 (over x, z_hi).
Axes of the slice: x: 4, y: 4, z: 4 (z_hi: 2, z_lo: 2; z = z_hi * 2 + z_lo), core: 2. Of those that a mesh axis runs over, the one named last changes fastest.
Arguments:
- llm_grad: bfloat16 [16384, 3072], P('tensor', 'dp'), may hold values from -6 to 6
- image_slot: int32 [64], replicated, may hold values from 0 to 63, each once
- pre_act: bfloat16 [16384, 12288], P('dp', 'tensor'), may hold values from -8 to 8
- w_down: bfloat16 [12288, 3072], P('tensor'), may hold values from -0.0546875 to 0.0546875
Outputs:
- grad_pre: bfloat16 [16384, 12288], P('dp', 'tensor')
- grad_down: float32 [12288, 3072], P('tensor', 'dp')
The draws below stay inside these ranges and needn't reach their ends.
Inputs may be any that keep to these rules, and one draw needn't show every extreme that they name: `image_slot`: each image slot is named by exactly one encoder image.
All inputs are finite; a program needn't handle non-finite values.
Results may differ from the reference program's by a relative error of at most 0.0027.
Values may be sent and summed in bfloat16 or wider, within the bound.
A program may use at most 128 MiB of HBM per device.

```python
import jax
import jax.numpy as jnp

D = 3072
FF = 12288
PATCH = 256
IMGS = 64
TOKENS = 16384


def spiked(drawn, own_key, source, target, blocks, factor):
    owner, partner = [(jnp.arange(drawn.shape[dim]) // (drawn.shape[dim] // blocks)).reshape([-1 if axis == dim else 1 for axis in range(drawn.ndim)]) for dim in (source, target)]
    chosen = jax.random.permutation(own_key, blocks)[partner]
    strong = (owner == chosen) | (owner == (partner + blocks // 2) % blocks)
    return jnp.where(strong, factor * drawn, drawn)


def steps_of(rng, shape, cuts, least, top_value):
    level, own = 1.0, jax.random.fold_in(rng, 6)
    for dim, shards_of in cuts:
        heights = jnp.exp(jax.random.uniform(jax.random.fold_in(own, dim), (shards_of,), jnp.float32, least / len(cuts), top_value / len(cuts)))
        level = level * jnp.repeat(heights, shape[dim] // shards_of).reshape([-1 if axis == dim else 1 for axis in range(len(shape))])
    return level


def gaussian(stream_key, extent, deviation, bound, pieces=(), held_as=jnp.bfloat16):
    drawn = jax.random.normal(stream_key, extent, jnp.float32) * deviation
    if len(pieces) > 0:
        drawn = steps_of(stream_key, extent, pieces, -0.22, 0.18) * drawn
    return jnp.clip(drawn, min=-bound, max=bound).astype(held_as)


def noise_with(own_key, dims, spread, reach, shards, heavy, held_as=jnp.bfloat16):
    array = spread * jax.random.normal(own_key, dims, jnp.float32)
    if shards:
        array = array * steps_of(own_key, dims, shards, -0.22, 0.18)
    return jnp.clip(spiked(array, jax.random.fold_in(own_key, 3), *heavy), -reach, reach).astype(held_as)


def setup_inputs(seed: int = 0) -> dict:
    splits = jax.random.split(jax.random.key(seed), 5)
    return {
        "llm_grad": noise_with(splits[0], (TOKENS, D), 1.0, 6.0, ((0, 8), (1, 16)), (0, 1, 16, 2.0)),
        "image_slot": jax.random.permutation(splits[1], IMGS).astype(jnp.int32),
        "pre_act": gaussian(splits[2], (TOKENS, FF), 1.5, 8.0, ((0, 16), (1, 8))),
        "w_down": gaussian(splits[3], (FF, D), FF ** -0.5, 0.0546875, ((0, 8),)),
    }


def gelu_parts(value):
    inner = 0.7978845608 * (value + 0.044715 * value * value * value)
    tanh_value = jnp.tanh(inner)
    out = 0.5 * value * (1.0 + tanh_value)
    slope = 0.5 * (1.0 + tanh_value) + 0.5 * value * (1.0 - tanh_value * tanh_value) * 0.7978845608 * (1.0 + 3.0 * 0.044715 * value * value)
    return (out, slope)

def reference(llm_grad, image_slot, pre_act, w_down):
    blocks = llm_grad.reshape(IMGS, PATCH, D)
    out_grad = blocks[image_slot].reshape(TOKENS, D)
    hidden_f, slope = gelu_parts(pre_act.astype(jnp.float32))
    hidden = hidden_f.astype(jnp.bfloat16)
    grad_hidden = jnp.dot(out_grad, w_down.T, preferred_element_type=jnp.float32)
    grad_pre = (grad_hidden * slope).astype(jnp.bfloat16)
    grad_down = jnp.dot(hidden.T, out_grad, preferred_element_type=jnp.float32) / jnp.sqrt(jnp.float32(TOKENS))
    return (grad_pre, grad_down)
```

```python
import jax
import jax.numpy as jnp
from jax import lax
from jax.experimental import pallas as pl
from jax.experimental.pallas import tpu as pltpu
from jax.sharding import PartitionSpec as P

MESH = pl.DeviceIdType.MESH
BF = jnp.bfloat16
F32 = jnp.float32
NK = 3
TOK = 1024
NF = 1536


def gelu_parts(value):
    inner = 0.7978845608 * (value + 0.044715 * value * value * value)
    tanh_value = jnp.tanh(inner)
    out = 0.5 * value * (1.0 + tanh_value)
    slope = 0.5 * (1.0 + tanh_value) + 0.5 * value * (
        1.0 - tanh_value * tanh_value
    ) * 0.7978845608 * (1.0 + 3.0 * 0.044715 * value * value)
    return (out, slope)


def kernel(
    slot_ref, llm_hbm, pre_hbm, w_hbm, gp_hbm, gd_hbm,
    llm, pre, w, send_t, recv_t0, recv_t1, recv_t2, send_d, own, sib, hid,
    left, acc, send_r, recv_r, mine, send_z, recv_z, fin, rhs, gp,
    in_sem, out_sem, t_ss, t_rs, d_ss, d_rs, g_ss, g_rs, s_ss, s_rs, h_ss, h_rs,
    r_ss, r_rs, z_ss, z_rs,
):
    recv_t = (recv_t0, recv_t1, recv_t2)
    dp = lax.axis_index("dp")
    j = lax.axis_index("tensor")
    y, zlo, c = dp // 4, (dp // 2) % 2, dp % 2
    x, zhi = j // 2, j % 2
    q = dp // 2

    def dev_t(o):
        return (dp, (j + o) % 8)

    def dev_q(o):
        return (((q + o) % 8) * 2 + c, j)

    sibling = (dp - c + (1 - c), j)
    z2 = (dp, 2 * x + (1 - zhi))
    xr, xl, xo = (x + 1) % 4, (x + 3) % 4, (x + 2) % 4
    dev_xr, dev_xl = (dp, 2 * xr + zhi), (dp, 2 * xl + zhi)
    zpart = ((y * 2 + (1 - zlo)) * 2 + c, j)

    def dev_y(o):
        return ((((y + o) % 4) * 2 + zlo) * 2 + c, j)

    def rcopy(src, dst, ss, rs, dev):
        return pltpu.make_async_remote_copy(
            src_ref=src, dst_ref=dst, send_sem=ss, recv_sem=rs, device_id=dev, device_id_type=MESH
        )

    sends = []

    def send(src, dst, ss, rs, dev):
        cp = rcopy(src, dst, ss, rs, dev)
        cp.start()
        sends.append(cp)

    def await_recv(land, ss, rs, dev):
        rcopy(land, land, ss, rs, dev).wait_recv()

    cp_llm = pltpu.make_async_copy(llm_hbm, llm, in_sem.at[0])
    cp_pre = pltpu.make_async_copy(pre_hbm, pre, in_sem.at[1])
    cp_w = pltpu.make_async_copy(w_hbm, w, in_sem.at[2])
    cp_llm.start()
    cp_pre.start()
    cp_w.start()
    barrier = pltpu.get_barrier_semaphore()
    for o in range(1, 8):
        pl.semaphore_signal(barrier, inc=1, device_id=dev_t(o), device_id_type=MESH)
        pl.semaphore_signal(barrier, inc=1, device_id=dev_q(o), device_id_type=MESH)
    pl.semaphore_signal(barrier, inc=1, device_id=sibling, device_id_type=MESH)
    cp_llm.wait()

    @pl.loop(0, 8)
    def _(s):
        for h in range(2):
            rows = pl.ds(pl.multiple_of(s * 256 + h * 128, 128), 128)
            flipped = llm[rows, :].T
            for cq in range(4):
                for k in range(NK):
                    send_t[k, cq * 2 + h, s] = flipped[48 * cq + 16 * k : 48 * cq + 16 * k + 16, :]

    pl.semaphore_wait(barrier, 15)

    def t_send(k):
        for o in range(1, 8):
            send(
                send_t.at[k, (j + o) % 8], recv_t[k].at[pl.ds(j * 8, 8)],
                t_ss.at[k, o], t_rs.at[k, o], dev_t(o),
            )
        recv_t[k][pl.ds(j * 8, 8)] = send_t[k, j]

    def t_wait_d_send(k):
        for o in range(1, 8):
            await_recv(recv_t[k].at[pl.ds(((j + 8 - o) % 8) * 8, 8)], t_ss.at[k, o], t_rs.at[k, o], dev_t(o))

        @pl.loop(0, 64)
        def _(e):
            send_d[k, e // 8, e % 8] = recv_t[k][slot_ref[e]]

        for o in range(1, 8):
            send(
                send_d.at[k, (q + o) % 8], own.at[k, j, q], d_ss.at[k, o], d_rs.at[k, o], dev_q(o)
            )
        own[k, j, q] = send_d[k, q]

    def d_wait(k):
        for o in range(1, 8):
            await_recv(own.at[k, j, (q + 8 - o) % 8], d_ss.at[k, o], d_rs.at[k, o], dev_q(o))

    def piece(k, xx, zz):
        return own.at[k, 2 * xx + zz]

    LO, HI = pl.ds(0, 4), pl.ds(4, 4)

    def half(k, xx, zz, part):
        return own.at[k, 2 * xx + zz, part]

    def g_send(k, n, ref, dev):
        send(ref, ref, g_ss.at[k, n], g_rs.at[k, n], dev)

    def g_wait(k, n, ref, dev):
        await_recv(ref, g_ss.at[k, n], g_rs.at[k, n], dev)

    oz = 1 - zhi

    def g_z(k):
        g_send(k, 0, piece(k, x, zhi), z2)

    def g_x(k):
        g_send(k, 1, piece(k, x, zhi), dev_xr)
        g_send(k, 2, piece(k, x, zhi), dev_xl)

    def g_b(k):
        g_wait(k, 0, piece(k, x, oz), z2)
        g_send(k, 3, piece(k, x, oz), dev_xr)
        g_send(k, 4, piece(k, x, oz), dev_xl)

    def g_c(k):
        g_wait(k, 1, piece(k, xl, zhi), dev_xl)
        g_send(k, 5, half(k, xl, zhi, LO), dev_xr)
        g_wait(k, 2, piece(k, xr, zhi), dev_xr)
        g_send(k, 6, half(k, xr, zhi, HI), dev_xl)

    def g_e(k):
        g_wait(k, 3, piece(k, xl, oz), dev_xl)
        g_send(k, 7, half(k, xl, oz, LO), dev_xr)
        g_wait(k, 4, piece(k, xr, oz), dev_xr)
        g_send(k, 8, half(k, xr, oz, HI), dev_xl)

    def g_f(k):
        g_wait(k, 5, half(k, xo, zhi, LO), dev_xl)
        g_wait(k, 6, half(k, xo, zhi, HI), dev_xr)
        g_wait(k, 7, half(k, xo, oz, LO), dev_xl)
        g_wait(k, 8, half(k, xo, oz, HI), dev_xr)
        send(
            own.at[k, :, :, pl.ds((1 - c) * 4, 4)], sib.at[k], s_ss.at[k], s_rs.at[k], sibling
        )

    def hidden_rows(first, count):
        @pl.loop(first, first + count)
        def _(b):
            rows = pl.ds(pl.multiple_of(b * 32, 32), 32)
            value, _ = gelu_parts(pre[rows, :].astype(F32))
            hid[pl.ds(pl.multiple_of(c * TOK + b * 32, 32), 32), :] = value.astype(BF)

    def down(k):
        @pl.loop(0, 8)
        def _(qq):
            for cq in range(4):
                row = pl.ds(pl.multiple_of(qq * 64 + cq * 16, 16), 16)
                for img in range(8):
                    for h in range(2):
                        left[row, (img * 2 + h) * 128 : (img * 2 + h + 1) * 128] = own[
                            k, cq * 2 + h, qq, img
                        ]

        @pl.loop(0, 6)
        def _(n):
            cols = pl.ds(pl.multiple_of(n * 256, 256), 256)
            part = jnp.dot(left[...], hid[:, cols], preferred_element_type=F32)
            part = part.reshape(8, 64, 256)
            acc[:, :, cols] = part
            send_r[k, :, :, cols] = part.astype(BF)

        for o in (2, 1, 3):
            send(
                send_r.at[k, pl.ds(((y + o) % 4) * 2, 2)], recv_r.at[k, o - 1],
                r_ss.at[k, o], r_rs.at[k, o], dev_y(o),
            )
        mine[k] = acc[pl.ds(y * 2, 2)]

    def r_sum(k):
        for o in (1, 2, 3):
            await_recv(recv_r.at[k, o - 1], r_ss.at[k, o], r_rs.at[k, o], dev_y(o))

        @pl.loop(0, 4)
        def _(b):
            rows = pl.ds(pl.multiple_of(b * 16, 16), 16)
            for side in range(2):
                zz = zlo if side == 0 else 1 - zlo
                total = mine[k, zz, rows, :]
                for o in range(3):
                    total += recv_r[k, o, zz, rows, :].astype(F32)
                if side == 0:
                    mine[k, zz, rows, :] = total
                else:
                    send_z[k, rows, :] = total.astype(BF)

        send(send_z.at[k], recv_z.at[k], z_ss.at[k], z_rs.at[k], zpart)

    def r_final(k):
        await_recv(recv_z.at[k], z_ss.at[k], z_rs.at[k], zpart)

        @pl.loop(0, 4)
        def _(cq):
            rows = pl.ds(pl.multiple_of(cq * 16, 16), 16)
            total = mine[k, zlo, rows, :] + recv_z[k, rows, :].astype(F32)
            fin[pl.ds(pl.multiple_of(cq * 48 + k * 16, 16), 16), :] = total * (1.0 / 128.0)

    def up(b):
        @pl.loop(0, 8)
        def _(qq):
            for cq in range(4):
                for k in range(NK):
                    for h in range(2):
                        lanes = slice(h * 128, (h + 1) * 128)
                        at = qq * 384 + cq * 48 + k * 16
                        rhs[pl.ds(pl.multiple_of(at + c * 192, 16), 16), lanes] = own[
                            k, cq * 2 + h, qq, c * 4 + b
                        ]
                        rhs[pl.ds(pl.multiple_of(at + (1 - c) * 192, 16), 16), lanes] = sib[
                            k, cq * 2 + h, qq, b
                        ]

        @pl.loop(0, 3)
        def _(n):
            fs = pl.ds(pl.multiple_of(n * 512, 512), 512)
            part = jnp.dot(w[fs, :], rhs[...], preferred_element_type=F32)
            _, slope = gelu_parts(pre[b * 256 : (b + 1) * 256, fs].astype(F32))
            gp[b * 256 : (b + 1) * 256, fs] = (part.T * slope).astype(BF)

        rows = pl.ds(b * 256, 256)
        cp = pltpu.make_async_copy(gp.at[rows], gp_hbm.at[rows], out_sem.at[b])
        cp.start()
        return cp

    t_send(0)
    t_send(1)
    t_send(2)
    cp_pre.wait()
    hidden_rows(0, 8)
    t_wait_d_send(0)
    t_wait_d_send(1)
    hidden_rows(8, 4)
    d_wait(0)
    g_z(0)
    g_x(0)
    t_wait_d_send(2)
    hidden_rows(12, 8)
    g_b(0)
    hidden_rows(20, 6)
    d_wait(1)
    g_z(1)
    g_c(0)
    hidden_rows(26, 6)
    send(
        hid.at[pl.ds(c * TOK, TOK)], hid.at[pl.ds(c * TOK, TOK)], h_ss.at[0], h_rs.at[0], sibling
    )
    g_e(0)
    g_x(1)
    g_b(1)
    d_wait(2)
    g_z(2)
    g_f(0)
    await_recv(hid.at[pl.ds((1 - c) * TOK, TOK)], h_ss.at[0], h_rs.at[0], sibling)
    down(0)
    g_c(1)
    g_e(1)
    g_x(2)
    g_b(2)
    g_f(1)
    down(1)
    g_c(2)
    g_e(2)
    r_sum(0)
    g_f(2)
    down(2)
    r_final(0)
    cp_w.wait()
    for k in range(NK):
        await_recv(sib.at[k], s_ss.at[k], s_rs.at[k], sibling)
    outs = [up(0)]
    r_sum(1)
    outs.append(up(1))
    outs.append(up(2))
    r_final(1)
    outs.append(up(3))
    r_sum(2)
    r_final(2)
    cp = pltpu.make_async_copy(fin, gd_hbm, out_sem.at[4])
    cp.start()
    outs.append(cp)
    for cp in outs:
        cp.wait()
    for cp in sends:
        cp.wait_send()


def on_device(llm_grad, image_slot, pre_act, w_down):
    dma = pltpu.SemaphoreType.DMA
    any_space = pl.BlockSpec(memory_space=pl.ANY)
    grad_pre, down = pl.pallas_call(
        kernel,
        out_shape=(
            jax.ShapeDtypeStruct((TOK, NF), BF),
            jax.ShapeDtypeStruct((192, NF), F32),
        ),
        in_specs=[pl.BlockSpec(memory_space=pltpu.SMEM), any_space, any_space, any_space],
        out_specs=(any_space, any_space),
        scratch_shapes=[
            pltpu.VMEM((2048, 192), BF),
            pltpu.VMEM((TOK, NF), BF),
            pltpu.VMEM((NF, 3072), BF),
            pltpu.VMEM((NK, 8, 8, 16, 128), BF),
            pltpu.VMEM((64, 16, 128), BF),
            pltpu.VMEM((64, 16, 128), BF),
            pltpu.VMEM((64, 16, 128), BF),
            pltpu.VMEM((NK, 8, 8, 16, 128), BF),
            pltpu.VMEM((NK, 8, 8, 8, 16, 128), BF),
            pltpu.VMEM((NK, 8, 8, 4, 16, 128), BF),
            pltpu.VMEM((2 * TOK, NF), BF),
            pltpu.VMEM((512, 2048), BF),
            pltpu.VMEM((8, 64, NF), F32),
            pltpu.VMEM((NK, 8, 64, NF), BF),
            pltpu.VMEM((NK, 3, 2, 64, NF), BF),
            pltpu.VMEM((NK, 2, 64, NF), F32),
            pltpu.VMEM((NK, 64, NF), BF),
            pltpu.VMEM((NK, 64, NF), BF),
            pltpu.VMEM((192, NF), F32),
            pltpu.VMEM((3072, 256), BF),
            pltpu.VMEM((TOK, NF), BF),
            dma((3,)), dma((5,)),
            dma((NK, 8)), dma((NK, 8)), dma((NK, 8)), dma((NK, 8)),
            dma((NK, 9)), dma((NK, 9)), dma((NK,)), dma((NK,)), dma((1,)), dma((1,)),
            dma((NK, 4)), dma((NK, 4)), dma((NK,)), dma((NK,)),
        ],
        compiler_params=pltpu.CompilerParams(
            collective_id=0, has_side_effects=True, vmem_limit_bytes=60 << 20
        ),
        cost_estimate=pl.CostEstimate(
            flops=19_327_352_832, bytes_accessed=18 << 20, transcendentals=3_000_000
        ),
    )(image_slot, llm_grad, pre_act, w_down)
    return (grad_pre, down.T)


def solution(mesh):
    placed = (P("tensor", "dp"), P(), P("dp", "tensor"), P("tensor", None))
    return jax.shard_map(
        on_device,
        mesh=mesh,
        in_specs=placed,
        out_specs=(P("dp", "tensor"), P("tensor", "dp")),
        check_vma=False,
    )
```

```python
import jax
import jax.numpy as jnp
from jax import lax
from jax.experimental import pallas as pl
from jax.experimental.pallas import tpu as pltpu
from jax.sharding import PartitionSpec as P

MESH = pl.DeviceIdType.MESH
BF = jnp.bfloat16
F32 = jnp.float32
NK = 3
TOK = 1024
NF = 1536
GROUPS = ((0, 6), (6, 6), (12, 6), (18, 4), (22, 2))
TO_Y = (3, 1)


def gelu_parts(value):
    inner = 0.7978845608 * (value + 0.044715 * value * value * value)
    tanh_value = jnp.tanh(inner)
    out = 0.5 * value * (1.0 + tanh_value)
    slope = 0.5 * (1.0 + tanh_value) + 0.5 * value * (
        1.0 - tanh_value * tanh_value
    ) * 0.7978845608 * (1.0 + 3.0 * 0.044715 * value * value)
    return (out, slope)


def kernel(
    slot_ref, llm_hbm, pre_hbm, w_hbm, pre, fin,
    llm, w, send_t, recv_t0, recv_t1, recv_t2, send_d, own, sib, hid,
    left, ghacc, send_r, recv_a, recv_r, mine, send_z, recv_z, rhs, slope,
    in_sem, out_sem, t_ss, t_rs, d_ss, d_rs, g_ss, g_rs, s_ss, s_rs, h_ss, h_rs,
    a_ss, a_rs, r_ss, r_rs, z_ss, z_rs,
):
    recv_t = (recv_t0, recv_t1, recv_t2)
    dp = lax.axis_index("dp")
    j = lax.axis_index("tensor")
    y, zlo, c = dp // 4, (dp // 2) % 2, dp % 2
    x, zhi = j // 2, j % 2
    q = dp // 2

    def dev_t(o):
        return (dp, (j + o) % 8)

    def dev_q(o):
        return (((q + o) % 8) * 2 + c, j)

    sibling = (dp - c + (1 - c), j)
    z2 = (dp, 2 * x + (1 - zhi))
    xr, xl, xo = (x + 1) % 4, (x + 3) % 4, (x + 2) % 4
    dev_xr, dev_xl = (dp, 2 * xr + zhi), (dp, 2 * xl + zhi)
    zpart = ((y * 2 + (1 - zlo)) * 2 + c, j)

    def dev_y(o):
        return ((((y + o) % 4) * 2 + zlo) * 2 + c, j)

    def rcopy(src, dst, ss, rs, dev):
        return pltpu.make_async_remote_copy(
            src_ref=src, dst_ref=dst, send_sem=ss, recv_sem=rs, device_id=dev, device_id_type=MESH
        )

    sends = []

    def send(src, dst, ss, rs, dev):
        cp = rcopy(src, dst, ss, rs, dev)
        cp.start()
        sends.append(cp)

    def await_recv(land, ss, rs, dev):
        rcopy(land, land, ss, rs, dev).wait_recv()

    cp_llm = pltpu.make_async_copy(llm_hbm, llm, in_sem.at[0])
    cp_pre = pltpu.make_async_copy(pre_hbm, pre, in_sem.at[1])
    cp_w = pltpu.make_async_copy(w_hbm, w, in_sem.at[2])
    cp_llm.start()
    cp_pre.start()
    cp_w.start()
    barrier = pltpu.get_barrier_semaphore()
    for o in range(1, 8):
        pl.semaphore_signal(barrier, inc=1, device_id=dev_t(o), device_id_type=MESH)
        pl.semaphore_signal(barrier, inc=1, device_id=dev_q(o), device_id_type=MESH)
    pl.semaphore_signal(barrier, inc=1, device_id=sibling, device_id_type=MESH)
    cp_llm.wait()

    @pl.loop(0, 8)
    def _(s):
        for h in range(2):
            lanes = pl.ds(pl.multiple_of(s * 256 + h * 128, 128), 128)
            for cq in range(4):
                for k in range(NK):
                    send_t[k, cq * 2 + h, s] = llm[48 * cq + 16 * k : 48 * cq + 16 * k + 16, lanes]

    pl.semaphore_wait(barrier, 15)

    def place(k, ys, yd, zl):
        off = (ys - yd + 4) % 4
        far = off // 2
        quarter = (1 - far) * (3 - off) + far * (off - 2)
        last = quarter // 3
        return last * (18 + 2 * k) + (1 - last) * (6 * k + 2 * quarter) + zl

    def t_send(k):
        for o in range(1, 8):
            send(
                send_t.at[k, (j + o) % 8], recv_t[k].at[pl.ds(j * 8, 8)],
                t_ss.at[k, o], t_rs.at[k, o], dev_t(o),
            )
        recv_t[k][pl.ds(j * 8, 8)] = send_t[k, j]

    def t_wait_d_send(k):
        for o in range(1, 8):
            await_recv(recv_t[k].at[pl.ds(((j + 8 - o) % 8) * 8, 8)], t_ss.at[k, o], t_rs.at[k, o], dev_t(o))

        @pl.loop(0, 64)
        def _(e):
            send_d[k, e // 8, e % 8] = recv_t[k][slot_ref[e]]

        for o in range(1, 8):
            qd = (q + o) % 8
            send(
                send_d.at[k, qd], own.at[j, place(k, y, qd // 2, zlo)],
                d_ss.at[k, o], d_rs.at[k, o], dev_q(o),
            )
        own[j, 18 + 2 * k + zlo] = send_d[k, q]

    def d_wait(k):
        for o in range(1, 8):
            qs = (q + 8 - o) % 8
            await_recv(
                own.at[j, place(k, qs // 2, y, qs % 2)], d_ss.at[k, o], d_rs.at[k, o], dev_q(o)
            )

    def piece(m, xx, zz):
        first, count = GROUPS[m]
        return own.at[2 * xx + zz, pl.ds(first, count)]

    def half(m, xx, zz, side):
        first, count = GROUPS[m]
        count //= 2
        return own.at[2 * xx + zz, pl.ds(first + side * count, count)]

    def g_send(m, n, ref, dev):
        send(ref, ref, g_ss.at[m, n], g_rs.at[m, n], dev)

    def g_wait(m, n, ref, dev):
        await_recv(ref, g_ss.at[m, n], g_rs.at[m, n], dev)

    oz = 1 - zhi

    def g_a(m):
        g_send(m, 0, piece(m, x, zhi), z2)
        g_send(m, 1, piece(m, x, zhi), dev_xr)
        g_send(m, 2, piece(m, x, zhi), dev_xl)

    def g_b(m):
        g_wait(m, 0, piece(m, x, oz), z2)
        g_send(m, 3, piece(m, x, oz), dev_xr)
        g_send(m, 4, piece(m, x, oz), dev_xl)

    def g_c(m):
        g_wait(m, 1, piece(m, xl, zhi), dev_xl)
        g_send(m, 5, half(m, xl, zhi, 0), dev_xr)
        g_wait(m, 2, piece(m, xr, zhi), dev_xr)
        g_send(m, 6, half(m, xr, zhi, 1), dev_xl)

    def g_e(m):
        g_wait(m, 3, piece(m, xl, oz), dev_xl)
        g_send(m, 7, half(m, xl, oz, 0), dev_xr)
        g_wait(m, 4, piece(m, xr, oz), dev_xr)
        g_send(m, 8, half(m, xr, oz, 1), dev_xl)

    def g_f(m):
        g_wait(m, 5, half(m, xo, zhi, 0), dev_xl)
        g_wait(m, 6, half(m, xo, zhi, 1), dev_xr)
        g_wait(m, 7, half(m, xo, oz, 0), dev_xl)
        g_wait(m, 8, half(m, xo, oz, 1), dev_xr)
        blocks = pl.ds(*GROUPS[m])
        send(
            own.at[:, blocks, pl.ds((1 - c) * 4, 4)], sib.at[:, blocks], s_ss.at[m], s_rs.at[m], sibling
        )

    def sib_wait(m):
        await_recv(sib.at[:, pl.ds(*GROUPS[m])], s_ss.at[m], s_rs.at[m], sibling)

    def hidden_rows(first, count):
        @pl.loop(first, first + count)
        def _(b):
            rows = pl.ds(pl.multiple_of(b * 32, 32), 32)
            value, slope_rows = gelu_parts(pre[rows, :].astype(F32))
            slope[rows, :] = slope_rows
            hid[pl.ds(pl.multiple_of(c * TOK + b * 32, 32), 32), :] = value.astype(BF)

    def down(first, count, store):
        @pl.loop(0, count)
        def _(qq):
            for cq in range(4):
                row = pl.ds(pl.multiple_of(qq * 64 + cq * 16, 16), 16)
                for img in range(8):
                    for h in range(2):
                        left[row, (img * 2 + h) * 128 : (img * 2 + h + 1) * 128] = own[
                            cq * 2 + h, first + qq, img
                        ]

        @pl.loop(0, 6)
        def _(n):
            cols = pl.ds(pl.multiple_of(n * 256, 256), 256)
            prod = jnp.dot(left[0 : count * 64, :], hid[:, cols], preferred_element_type=F32)
            prod = prod.reshape(count, 64, 256)
            for at in range(count):
                store(at, cols, prod[at])

    def down_a(k):
        def store(at, cols, rows):
            send_r[k, at, :, cols] = rows.astype(BF)

        down(6 * k, 2, store)
        for n in range(2):
            send(send_r.at[k, n], recv_a.at[k, n], a_ss.at[k, n], a_rs.at[k, n], dev_y(1 + 2 * n))

    def down_b(k):
        for n in range(2):
            await_recv(recv_a.at[k, n], a_ss.at[k, n], a_rs.at[k, n], dev_y(3 - 2 * n))

        def store(at, cols, rows):
            if at in (1, 2):
                rows += recv_a[k, 2 - at, :, cols].astype(F32)
            send_r[k, 2 + at, :, cols] = rows.astype(BF)

        down(6 * k + 2, 4, store)
        for n in range(2):
            send(
                send_r.at[k, pl.ds(2 + 2 * n, 2)], recv_r.at[k, n],
                r_ss.at[k, n], r_rs.at[k, n], dev_y(TO_Y[n]),
            )

    def down_c(k, chunks):
        def store(at, cols, rows):
            mine[k + at // 2, at % 2, :, cols] = rows

        down(18 + 2 * k, 2 * chunks, store)

    def r_sum(k):
        for n in range(2):
            await_recv(recv_r.at[k, n], r_ss.at[k, n], r_rs.at[k, n], dev_y(TO_Y[1 - n]))

        @pl.loop(0, 4)
        def _(b):
            rows = pl.ds(pl.multiple_of(b * 16, 16), 16)
            for side in range(2):
                zz = zlo if side == 0 else 1 - zlo
                total = mine[k, zz, rows, :]
                for o in range(2):
                    total += recv_r[k, o, zz, rows, :].astype(F32)
                if side == 0:
                    mine[k, zz, rows, :] = total
                else:
                    send_z[k, rows, :] = total.astype(BF)

        send(send_z.at[k], recv_z.at[k], z_ss.at[k], z_rs.at[k], zpart)

    def r_final(k):
        await_recv(recv_z.at[k], z_ss.at[k], z_rs.at[k], zpart)

        @pl.loop(0, 4)
        def _(cq):
            rows = pl.ds(pl.multiple_of(cq * 16, 16), 16)
            total = mine[k, zlo, rows, :] + recv_z[k, rows, :].astype(F32)
            fin[pl.ds(pl.multiple_of(cq * 48 + k * 16, 16), 16), :] = total * (1.0 / 128.0)

    def order_w(b):
        rows = pl.ds(b * 256, 256)
        out = lax.broadcasted_iota(jnp.int32, (384, 384), 1)
        source = ((out >> 6) & 1) * 192 + ((out >> 4) & 3) * 48 + (out >> 7) * 16 + (out & 15)
        perm = (lax.broadcasted_iota(jnp.int32, (384, 384), 0) == source).astype(F32).astype(BF)

        @pl.loop(0, 8)
        def _(u):
            cols = pl.ds(pl.multiple_of(u * 384, 384), 384)
            w[rows, cols] = jnp.dot(w[rows, cols], perm, preferred_element_type=F32).astype(BF)

    def up(g, b):
        def source(at):
            if g < 3:
                return g, 2 * ((y + (2, 3, 1)[at // 2]) % 4) + at % 2
            return at // 2, 2 * y + at % 2

        for at in range(6):
            for cq in range(4):
                for h in range(2):
                    lanes = slice(h * 128, (h + 1) * 128)
                    for p, rows in (
                        (c, own[cq * 2 + h, 6 * g + at, c * 4 + b]),
                        (1 - c, sib[cq * 2 + h, 6 * g + at, b]),
                    ):
                        row = pl.multiple_of(at * 128 + p * 64 + cq * 16, 16)
                        rhs[pl.ds(row, 16), lanes] = rows

        tokens = slice(b * 256, (b + 1) * 256)

        @pl.loop(0, 3)
        def _(n):
            fs = pl.ds(pl.multiple_of(n * 512, 512), 512)
            blocks = []
            for at in range(6):
                k, qq = source(at)
                blocks.append(w[fs, pl.ds(pl.multiple_of(qq * 384 + k * 128, 128), 128)])
            lhs = jnp.concatenate(blocks, axis=1)
            part = jnp.dot(lhs, rhs[...], preferred_element_type=F32)
            if g > 0:
                part += ghacc[fs, tokens]
            if g < 3:
                ghacc[fs, tokens] = part
            else:
                pre[tokens, fs] = (part.T * slope[tokens, fs]).astype(BF)


    t_send(0)
    cp_pre.wait()
    hidden_rows(0, 16)
    t_wait_d_send(0)
    t_send(1)
    t_send(2)
    cp_w.wait()
    order_w(0)
    d_wait(0)
    g_a(0)
    t_wait_d_send(1)
    hidden_rows(16, 4)
    g_b(0)
    t_wait_d_send(2)
    hidden_rows(20, 6)
    g_c(0)
    hidden_rows(26, 6)
    send(hid.at[pl.ds(c * TOK, TOK)], hid.at[pl.ds(c * TOK, TOK)], h_ss.at[0], h_rs.at[0], sibling)
    g_e(0)
    d_wait(1)
    g_a(1)
    order_w(1)
    order_w(2)
    g_b(1)
    g_f(0)
    await_recv(hid.at[pl.ds((1 - c) * TOK, TOK)], h_ss.at[0], h_rs.at[0], sibling)
    down_a(0)
    g_c(1)
    d_wait(2)
    g_a(2)
    order_w(3)
    order_w(4)
    order_w(5)
    g_e(1)
    g_b(2)
    down_b(0)
    sib_wait(0)
    up(0, 0)
    up(0, 1)
    g_f(1)
    down_a(1)
    g_c(2)
    g_a(3)
    up(0, 2)
    up(0, 3)
    sib_wait(1)
    up(1, 0)
    g_e(2)
    g_b(3)
    down_b(1)
    up(1, 1)
    up(1, 2)
    g_f(2)
    down_a(2)
    g_c(3)
    g_a(4)
    g_e(3)
    g_b(4)
    sib_wait(2)
    up(1, 3)
    up(2, 0)
    g_c(4)
    up(2, 1)
    g_f(3)
    g_e(4)
    down_b(2)
    down_c(0, 2)
    r_sum(0)
    r_sum(1)
    g_f(4)
    down_c(2, 1)
    r_sum(2)
    up(2, 2)
    up(2, 3)
    r_final(0)
    sib_wait(3)
    sib_wait(4)
    up(3, 0)
    r_final(1)
    up(3, 1)
    r_final(2)
    up(3, 2)
    up(3, 3)
    for cp in sends:
        cp.wait_send()


def on_device(llm_grad, image_slot, pre_act, w_down):
    dma = pltpu.SemaphoreType.DMA
    any_space = pl.BlockSpec(memory_space=pl.ANY)
    grad_pre, down = pl.pallas_call(
        kernel,
        out_shape=(
            pltpu.VMEM((TOK, NF), BF),
            pltpu.VMEM((192, NF), F32),
        ),
        in_specs=[pl.BlockSpec(memory_space=pltpu.SMEM), any_space, any_space, any_space],
        out_specs=(pl.BlockSpec(memory_space=pltpu.VMEM), pl.BlockSpec(memory_space=pltpu.VMEM)),
        scratch_shapes=[
            pltpu.VMEM((192, 2048), BF),
            pltpu.VMEM((NF, 3072), BF),
            pltpu.VMEM((NK, 8, 8, 16, 128), BF),
            pltpu.VMEM((64, 16, 128), BF),
            pltpu.VMEM((64, 16, 128), BF),
            pltpu.VMEM((64, 16, 128), BF),
            pltpu.VMEM((NK, 8, 8, 16, 128), BF),
            pltpu.VMEM((8, 24, 8, 16, 128), BF),
            pltpu.VMEM((8, 24, 4, 16, 128), BF),
            pltpu.VMEM((2 * TOK, NF), BF),
            pltpu.VMEM((256, 2048), BF),
            pltpu.VMEM((NF, TOK), F32),
            pltpu.VMEM((NK, 6, 64, NF), BF),
            pltpu.VMEM((NK, 2, 64, NF), BF),
            pltpu.VMEM((NK, 2, 2, 64, NF), BF),
            pltpu.VMEM((NK, 2, 64, NF), F32),
            pltpu.VMEM((NK, 64, NF), BF),
            pltpu.VMEM((NK, 64, NF), BF),
            pltpu.VMEM((768, 256), BF),
            pltpu.VMEM((TOK, NF), F32),
            dma((3,)), dma((1,)),
            dma((NK, 8)), dma((NK, 8)), dma((NK, 8)), dma((NK, 8)),
            dma((5, 9)), dma((5, 9)), dma((5,)), dma((5,)), dma((1,)), dma((1,)),
            dma((NK, 2)), dma((NK, 2)), dma((NK, 2)), dma((NK, 2)), dma((NK,)), dma((NK,)),
        ],
        compiler_params=pltpu.CompilerParams(
            collective_id=0, has_side_effects=True, vmem_limit_bytes=56 << 20
        ),
        cost_estimate=pl.CostEstimate(
            flops=19_327_352_832, bytes_accessed=18 << 20, transcendentals=3_000_000
        ),
    )(image_slot, llm_grad.T, pre_act, w_down)
    return (grad_pre, down.T)


def solution(mesh):
    placed = (P("tensor", "dp"), P(), P("dp", "tensor"), P("tensor", None))
    return jax.shard_map(
        on_device,
        mesh=mesh,
        in_specs=placed,
        out_specs=(P("dp", "tensor"), P("tensor", "dp")),
        check_vma=False,
    )
```

```python
import jax
import jax.numpy as jnp
from jax import lax
from jax.experimental import pallas as pl
from jax.experimental.pallas import tpu as pltpu
from jax.sharding import PartitionSpec as P

MESH = pl.DeviceIdType.MESH
BF = jnp.bfloat16
F32 = jnp.float32
NK = 3
TOK = 1024
NF = 1536
GROUPS = ((0, 6), (6, 6), (12, 6), (18, 4), (22, 2))
TO_Y = (3, 1)


def gelu_parts(value):
    inner = 0.7978845608 * (value + 0.044715 * value * value * value)
    tanh_value = jnp.tanh(inner)
    out = 0.5 * value * (1.0 + tanh_value)
    slope = 0.5 * (1.0 + tanh_value) + 0.5 * value * (
        1.0 - tanh_value * tanh_value
    ) * 0.7978845608 * (1.0 + 3.0 * 0.044715 * value * value)
    return (out, slope)


def kernel(
    slot_ref, llm_hbm, pre_hbm, w_hbm, pre, fin,
    llm, w, send_t, recv_t0, recv_t1, recv_t2, send_d, own, sib, hid,
    left, ghacc, send_r, wait_r, recv_a, recv_r, mine, send_z, recv_z, rhs, slope,
    in_sem, out_sem, t_ss, t_rs, d_ss, d_rs, g_ss, g_rs, s_ss, s_rs, h_ss, h_rs,
    a_ss, a_rs, r_ss, r_rs, z_ss, z_rs,
):
    recv_t = (recv_t0, recv_t1, recv_t2)
    dp = lax.axis_index("dp")
    j = lax.axis_index("tensor")
    y, zlo, c = dp // 4, (dp // 2) % 2, dp % 2
    x, zhi = j // 2, j % 2
    q = dp // 2

    def dev_t(o):
        return (dp, (j + o) % 8)

    def dev_q(o):
        return (((q + o) % 8) * 2 + c, j)

    sibling = (dp - c + (1 - c), j)
    z2 = (dp, 2 * x + (1 - zhi))
    xr, xl, xo = (x + 1) % 4, (x + 3) % 4, (x + 2) % 4
    dev_xr, dev_xl = (dp, 2 * xr + zhi), (dp, 2 * xl + zhi)
    zpart = ((y * 2 + (1 - zlo)) * 2 + c, j)

    def dev_y(o):
        return ((((y + o) % 4) * 2 + zlo) * 2 + c, j)

    def rcopy(src, dst, ss, rs, dev):
        return pltpu.make_async_remote_copy(
            src_ref=src, dst_ref=dst, send_sem=ss, recv_sem=rs, device_id=dev, device_id_type=MESH
        )

    sends = []

    def send(src, dst, ss, rs, dev):
        cp = rcopy(src, dst, ss, rs, dev)
        cp.start()
        sends.append(cp)

    def await_recv(land, ss, rs, dev):
        rcopy(land, land, ss, rs, dev).wait_recv()

    cp_llm = pltpu.make_async_copy(llm_hbm, llm, in_sem.at[0])
    cp_pre = pltpu.make_async_copy(pre_hbm, pre, in_sem.at[1])
    cp_w = pltpu.make_async_copy(w_hbm, w, in_sem.at[2])
    cp_llm.start()
    cp_pre.start()
    cp_w.start()
    barrier = pltpu.get_barrier_semaphore()
    for o in range(1, 8):
        pl.semaphore_signal(barrier, inc=1, device_id=dev_t(o), device_id_type=MESH)
        pl.semaphore_signal(barrier, inc=1, device_id=dev_q(o), device_id_type=MESH)
    pl.semaphore_signal(barrier, inc=1, device_id=sibling, device_id_type=MESH)
    cp_llm.wait()

    @pl.loop(0, 8)
    def _(s):
        for h in range(2):
            lanes = pl.ds(pl.multiple_of(s * 256 + h * 128, 128), 128)
            for cq in range(4):
                for k in range(NK):
                    send_t[k, cq * 2 + h, s] = llm[48 * cq + 16 * k : 48 * cq + 16 * k + 16, lanes]

    pl.semaphore_wait(barrier, 15)

    def place(k, ys, yd, zl):
        off = (ys - yd + 4) % 4
        far = off // 2
        quarter = (1 - far) * (3 - off) + far * (off - 2)
        last = quarter // 3
        return last * (18 + 2 * k) + (1 - last) * (6 * k + 2 * quarter) + zl

    def t_send(k):
        for o in range(1, 8):
            send(
                send_t.at[k, (j + o) % 8], recv_t[k].at[pl.ds(j * 8, 8)],
                t_ss.at[k, o], t_rs.at[k, o], dev_t(o),
            )
        recv_t[k][pl.ds(j * 8, 8)] = send_t[k, j]

    def t_wait_d_send(k):
        for o in range(1, 8):
            await_recv(recv_t[k].at[pl.ds(((j + 8 - o) % 8) * 8, 8)], t_ss.at[k, o], t_rs.at[k, o], dev_t(o))

        @pl.loop(0, 64)
        def _(e):
            send_d[k, e // 8, e % 8] = recv_t[k][slot_ref[e]]

        for o in range(1, 8):
            qd = (q + o) % 8
            send(
                send_d.at[k, qd], own.at[j, place(k, y, qd // 2, zlo)],
                d_ss.at[k, o], d_rs.at[k, o], dev_q(o),
            )
        own[j, 18 + 2 * k + zlo] = send_d[k, q]

    def d_wait(k):
        for o in range(1, 8):
            qs = (q + 8 - o) % 8
            await_recv(
                own.at[j, place(k, qs // 2, y, qs % 2)], d_ss.at[k, o], d_rs.at[k, o], dev_q(o)
            )

    def piece(m, xx, zz):
        first, count = GROUPS[m]
        return own.at[2 * xx + zz, pl.ds(first, count)]

    def half(m, xx, zz, side):
        first, count = GROUPS[m]
        count //= 2
        return own.at[2 * xx + zz, pl.ds(first + side * count, count)]

    def g_send(m, n, ref, dev):
        send(ref, ref, g_ss.at[m, n], g_rs.at[m, n], dev)

    def g_wait(m, n, ref, dev):
        await_recv(ref, g_ss.at[m, n], g_rs.at[m, n], dev)

    oz = 1 - zhi

    def g_a(m):
        g_send(m, 0, piece(m, x, zhi), z2)
        g_send(m, 1, piece(m, x, zhi), dev_xr)
        g_send(m, 2, piece(m, x, zhi), dev_xl)

    def g_b(m):
        g_wait(m, 0, piece(m, x, oz), z2)
        g_send(m, 3, piece(m, x, oz), dev_xr)
        g_send(m, 4, piece(m, x, oz), dev_xl)

    def g_c(m):
        g_wait(m, 1, piece(m, xl, zhi), dev_xl)
        g_send(m, 5, half(m, xl, zhi, 0), dev_xr)
        g_wait(m, 2, piece(m, xr, zhi), dev_xr)
        g_send(m, 6, half(m, xr, zhi, 1), dev_xl)

    def g_e(m):
        g_wait(m, 3, piece(m, xl, oz), dev_xl)
        g_send(m, 7, half(m, xl, oz, 0), dev_xr)
        g_wait(m, 4, piece(m, xr, oz), dev_xr)
        g_send(m, 8, half(m, xr, oz, 1), dev_xl)

    def g_f(m):
        g_wait(m, 5, half(m, xo, zhi, 0), dev_xl)
        g_wait(m, 6, half(m, xo, zhi, 1), dev_xr)
        g_wait(m, 7, half(m, xo, oz, 0), dev_xl)
        g_wait(m, 8, half(m, xo, oz, 1), dev_xr)
        blocks = pl.ds(*GROUPS[m])
        send(
            own.at[:, blocks, pl.ds((1 - c) * 4, 4)], sib.at[:, blocks], s_ss.at[m], s_rs.at[m], sibling
        )

    def sib_wait(m):
        await_recv(sib.at[:, pl.ds(*GROUPS[m])], s_ss.at[m], s_rs.at[m], sibling)

    def hidden_rows(first, count):
        @pl.loop(first, first + count)
        def _(b):
            rows = pl.ds(pl.multiple_of(b * 32, 32), 32)
            value, slope_rows = gelu_parts(pre[rows, :].astype(F32))
            slope[rows, :] = slope_rows
            hid[pl.ds(pl.multiple_of(c * TOK + b * 32, 32), 32), :] = value.astype(BF)

    def down(first, count, store):
        @pl.loop(0, count)
        def _(qq):
            for cq in range(4):
                row = pl.ds(pl.multiple_of(qq * 64 + cq * 16, 16), 16)
                for img in range(8):
                    for h in range(2):
                        left[row, (img * 2 + h) * 128 : (img * 2 + h + 1) * 128] = own[
                            cq * 2 + h, first + qq, img
                        ]

        @pl.loop(0, 2)
        def _(n):
            cols = pl.ds(pl.multiple_of(n * 768, 768), 768)
            prod = jnp.dot(left[0 : count * 64, :], hid[:, cols], preferred_element_type=F32)
            prod = prod.reshape(count, 64, 768)
            for at in range(count):
                store(at, cols, prod[at])

    def down_a(k):
        def store(at, cols, rows):
            send_r[k, at, :, cols] = rows.astype(BF)

        down(6 * k, 2, store)
        for n in range(2):
            send(send_r.at[k, n], recv_a.at[k, n], a_ss.at[k, n], a_rs.at[k, n], dev_y(1 + 2 * n))

    def r_send(k, at):
        n, zz = at // 2, at % 2
        send(
            send_r.at[k, 2 + at], recv_r.at[k, n, zz], r_ss.at[k, at], r_rs.at[k, at], dev_y(TO_Y[n])
        )

    def down_b(k):
        def store(at, cols, rows):
            if at in (1, 2):
                wait_r[at - 1, :, cols] = rows
            else:
                send_r[k, 2 + at, :, cols] = rows.astype(BF)

        down(6 * k + 2, 4, store)
        r_send(k, 0)
        r_send(k, 3)

    def relay(k):
        for n in range(2):
            await_recv(recv_a.at[k, n], a_ss.at[k, n], a_rs.at[k, n], dev_y(3 - 2 * n))

        @pl.loop(0, 4)
        def _(b):
            rows = pl.ds(pl.multiple_of(b * 16, 16), 16)
            for n in range(2):
                total = wait_r[n, rows, :] + recv_a[k, 1 - n, rows, :].astype(F32)
                send_r[k, 3 + n, rows, :] = total.astype(BF)

        r_send(k, 1)
        r_send(k, 2)

    def down_c(k, chunks):
        def store(at, cols, rows):
            mine[k + at // 2, at % 2, :, cols] = rows

        down(18 + 2 * k, 2 * chunks, store)

    def r_sum(k):
        for at in range(4):
            n, zz = at // 2, at % 2
            await_recv(recv_r.at[k, n, zz], r_ss.at[k, at], r_rs.at[k, at], dev_y(TO_Y[1 - n]))

        @pl.loop(0, 4)
        def _(b):
            rows = pl.ds(pl.multiple_of(b * 16, 16), 16)
            for side in range(2):
                zz = zlo if side == 0 else 1 - zlo
                total = mine[k, zz, rows, :]
                for o in range(2):
                    total += recv_r[k, o, zz, rows, :].astype(F32)
                if side == 0:
                    mine[k, zz, rows, :] = total
                else:
                    send_z[k, rows, :] = total.astype(BF)

        send(send_z.at[k], recv_z.at[k], z_ss.at[k], z_rs.at[k], zpart)

    def r_final(k):
        await_recv(recv_z.at[k], z_ss.at[k], z_rs.at[k], zpart)

        @pl.loop(0, 4)
        def _(cq):
            rows = pl.ds(pl.multiple_of(cq * 16, 16), 16)
            total = mine[k, zlo, rows, :] + recv_z[k, rows, :].astype(F32)
            fin[pl.ds(pl.multiple_of(cq * 48 + k * 16, 16), 16), :] = total * (1.0 / 128.0)

    def order_w(b):
        rows = pl.ds(b * 512, 512)
        out = lax.broadcasted_iota(jnp.int32, (384, 384), 1)
        source = ((out >> 6) & 1) * 192 + ((out >> 4) & 3) * 48 + (out >> 7) * 16 + (out & 15)
        perm = (lax.broadcasted_iota(jnp.int32, (384, 384), 0) == source).astype(F32).astype(BF)

        @pl.loop(0, 8)
        def _(u):
            cols = pl.ds(pl.multiple_of(u * 384, 384), 384)
            w[rows, cols] = jnp.dot(w[rows, cols], perm, preferred_element_type=F32).astype(BF)

    def up(g, b):
        first, count = GROUPS[g]

        def source(at):
            if g < 3:
                return g, 2 * ((y + (2, 3, 1)[at // 2]) % 4) + at % 2
            return 2 * (g - 3) + at // 2, 2 * y + at % 2

        for at in range(count):
            for cq in range(4):
                for n in range(4):
                    lanes = slice(n * 128, (n + 1) * 128)
                    img, h = 2 * b + n // 2, n % 2
                    for p, rows in (
                        (c, own[cq * 2 + h, first + at, c * 4 + img]),
                        (1 - c, sib[cq * 2 + h, first + at, img]),
                    ):
                        row = pl.multiple_of(at * 128 + p * 64 + cq * 16, 16)
                        rhs[pl.ds(row, 16), lanes] = rows

        tokens = slice(b * 512, (b + 1) * 512)

        @pl.loop(0, 2)
        def _(n):
            fs = pl.ds(pl.multiple_of(n * 768, 768), 768)
            blocks = []
            for at in range(count):
                k, qq = source(at)
                blocks.append(w[fs, pl.ds(pl.multiple_of(qq * 384 + k * 128, 128), 128)])
            lhs = jnp.concatenate(blocks, axis=1)
            part = jnp.dot(lhs, rhs[0 : count * 128, :], preferred_element_type=F32)
            if g > 0:
                part += ghacc[fs, tokens]
            if g < 4:
                ghacc[fs, tokens] = part
            else:
                pre[tokens, fs] = (part.T * slope[tokens, fs]).astype(BF)


    t_send(0)
    cp_pre.wait()
    hidden_rows(0, 16)
    t_wait_d_send(0)
    t_send(1)
    t_send(2)
    cp_w.wait()
    order_w(0)
    d_wait(0)
    g_a(0)
    t_wait_d_send(1)
    hidden_rows(16, 4)
    g_b(0)
    t_wait_d_send(2)
    hidden_rows(20, 6)
    g_c(0)
    hidden_rows(26, 6)
    send(hid.at[pl.ds(c * TOK, TOK)], hid.at[pl.ds(c * TOK, TOK)], h_ss.at[0], h_rs.at[0], sibling)
    g_e(0)
    d_wait(1)
    g_a(1)
    order_w(1)
    g_b(1)
    g_f(0)
    await_recv(hid.at[pl.ds((1 - c) * TOK, TOK)], h_ss.at[0], h_rs.at[0], sibling)
    down_a(0)
    g_c(1)
    d_wait(2)
    g_a(2)
    down_b(0)
    order_w(2)
    g_e(1)
    g_b(2)
    relay(0)
    sib_wait(0)
    up(0, 0)
    g_f(1)
    down_a(1)
    g_c(2)
    g_a(3)
    down_b(1)
    up(0, 1)
    g_e(2)
    g_b(3)
    relay(1)
    sib_wait(1)
    up(1, 0)
    up(1, 1)
    g_f(2)
    down_a(2)
    g_c(3)
    g_a(4)
    down_b(2)
    g_e(3)
    g_b(4)
    g_c(4)
    relay(2)
    sib_wait(2)
    up(2, 0)
    g_f(3)
    g_e(4)
    down_c(0, 2)
    r_sum(0)
    r_sum(1)
    sib_wait(3)
    up(2, 1)
    up(3, 0)
    g_f(4)
    down_c(2, 1)
    r_sum(2)
    up(3, 1)
    r_final(0)
    r_final(1)
    sib_wait(4)
    up(4, 0)
    r_final(2)
    up(4, 1)
    for cp in sends:
        cp.wait_send()


def on_device(llm_grad, image_slot, pre_act, w_down):
    dma = pltpu.SemaphoreType.DMA
    any_space = pl.BlockSpec(memory_space=pl.ANY)
    grad_pre, down = pl.pallas_call(
        kernel,
        out_shape=(
            pltpu.VMEM((TOK, NF), BF),
            pltpu.VMEM((192, NF), F32),
        ),
        in_specs=[pl.BlockSpec(memory_space=pltpu.SMEM), any_space, any_space, any_space],
        out_specs=(pl.BlockSpec(memory_space=pltpu.VMEM), pl.BlockSpec(memory_space=pltpu.VMEM)),
        scratch_shapes=[
            pltpu.VMEM((192, 2048), BF),
            pltpu.VMEM((NF, 3072), BF),
            pltpu.VMEM((NK, 8, 8, 16, 128), BF),
            pltpu.VMEM((64, 16, 128), BF),
            pltpu.VMEM((64, 16, 128), BF),
            pltpu.VMEM((64, 16, 128), BF),
            pltpu.VMEM((NK, 8, 8, 16, 128), BF),
            pltpu.VMEM((8, 24, 8, 16, 128), BF),
            pltpu.VMEM((8, 24, 4, 16, 128), BF),
            pltpu.VMEM((2 * TOK, NF), BF),
            pltpu.VMEM((256, 2048), BF),
            pltpu.VMEM((NF, TOK), F32),
            pltpu.VMEM((NK, 6, 64, NF), BF),
            pltpu.VMEM((2, 64, NF), F32),
            pltpu.VMEM((NK, 2, 64, NF), BF),
            pltpu.VMEM((NK, 2, 2, 64, NF), BF),
            pltpu.VMEM((NK, 2, 64, NF), F32),
            pltpu.VMEM((NK, 64, NF), BF),
            pltpu.VMEM((NK, 64, NF), BF),
            pltpu.VMEM((768, 512), BF),
            pltpu.VMEM((TOK, NF), F32),
            dma((3,)), dma((1,)),
            dma((NK, 8)), dma((NK, 8)), dma((NK, 8)), dma((NK, 8)),
            dma((5, 9)), dma((5, 9)), dma((5,)), dma((5,)), dma((1,)), dma((1,)),
            dma((NK, 2)), dma((NK, 2)), dma((NK, 4)), dma((NK, 4)), dma((NK,)), dma((NK,)),
        ],
        compiler_params=pltpu.CompilerParams(
            collective_id=0, has_side_effects=True, vmem_limit_bytes=56 << 20
        ),
        cost_estimate=pl.CostEstimate(
            flops=19_327_352_832, bytes_accessed=18 << 20, transcendentals=3_000_000
        ),
    )(image_slot, llm_grad.T, pre_act, w_down)
    return (grad_pre, down.T)


def solution(mesh):
    placed = (P("tensor", "dp"), P(), P("dp", "tensor"), P("tensor", None))
    return jax.shard_map(
        on_device,
        mesh=mesh,
        in_specs=placed,
        out_specs=(P("dp", "tensor"), P("tensor", "dp")),
        check_vma=False,
    )
```

```python
import jax
import jax.numpy as jnp
from jax import lax
from jax.experimental import pallas as pl
from jax.experimental.pallas import tpu as pltpu
from jax.sharding import PartitionSpec as P

MESH = pl.DeviceIdType.MESH
BF = jnp.bfloat16
F32 = jnp.float32
NK = 3
TOK = 1024
NF = 1536
GROUPS = ((0, 6), (6, 6), (12, 6), (18, 4), (22, 2))
TO_Y = (3, 1)


def gelu_parts(value):
    inner = 0.7978845608 * (value + 0.044715 * value * value * value)
    tanh_value = jnp.tanh(inner)
    out = 0.5 * value * (1.0 + tanh_value)
    slope = 0.5 * (1.0 + tanh_value) + 0.5 * value * (
        1.0 - tanh_value * tanh_value
    ) * 0.7978845608 * (1.0 + 3.0 * 0.044715 * value * value)
    return (out, slope)


def kernel(
    slot_ref, llm_hbm, pre_hbm, w_hbm, pre, fin,
    llm, w, send_t, recv_t0, recv_t1, recv_t2, send_d, own, sib, hid,
    left, ghacc, send_r, wait_r, recv_a, recv_r, mine, send_z, recv_z, rhs, slope,
    in_sem, out_sem, t_ss, t_rs, d_ss, d_rs, g_ss, g_rs, s_ss, s_rs, h_ss, h_rs,
    a_ss, a_rs, r_ss, r_rs, z_ss, z_rs,
):
    recv_t = (recv_t0, recv_t1, recv_t2)
    dp = lax.axis_index("dp")
    j = lax.axis_index("tensor")
    y, zlo, c = dp // 4, (dp // 2) % 2, dp % 2
    x, zhi = j // 2, j % 2
    q = dp // 2

    def dev_t(o):
        return (dp, (j + o) % 8)

    def dev_q(o):
        return (((q + o) % 8) * 2 + c, j)

    sibling = (dp - c + (1 - c), j)
    z2 = (dp, 2 * x + (1 - zhi))
    xr, xl, xo = (x + 1) % 4, (x + 3) % 4, (x + 2) % 4
    dev_xr, dev_xl = (dp, 2 * xr + zhi), (dp, 2 * xl + zhi)
    zpart = ((y * 2 + (1 - zlo)) * 2 + c, j)

    def dev_y(o):
        return ((((y + o) % 4) * 2 + zlo) * 2 + c, j)

    def rcopy(src, dst, ss, rs, dev):
        return pltpu.make_async_remote_copy(
            src_ref=src, dst_ref=dst, send_sem=ss, recv_sem=rs, device_id=dev, device_id_type=MESH
        )

    sends = []

    def send(src, dst, ss, rs, dev):
        cp = rcopy(src, dst, ss, rs, dev)
        cp.start()
        sends.append(cp)

    def await_recv(land, ss, rs, dev):
        rcopy(land, land, ss, rs, dev).wait_recv()

    cp_llm = pltpu.make_async_copy(llm_hbm, llm, in_sem.at[0])
    cp_pre = pltpu.make_async_copy(pre_hbm, pre, in_sem.at[1])
    cp_w = pltpu.make_async_copy(w_hbm, w, in_sem.at[2])
    cp_llm.start()
    cp_pre.start()
    cp_w.start()
    barrier = pltpu.get_barrier_semaphore()
    for o in range(1, 8):
        pl.semaphore_signal(barrier, inc=1, device_id=dev_t(o), device_id_type=MESH)
        pl.semaphore_signal(barrier, inc=1, device_id=dev_q(o), device_id_type=MESH)
    pl.semaphore_signal(barrier, inc=1, device_id=sibling, device_id_type=MESH)
    cp_llm.wait()

    @pl.loop(0, 8)
    def _(s):
        for h in range(2):
            lanes = pl.ds(pl.multiple_of(s * 256 + h * 128, 128), 128)
            for cq in range(4):
                for k in range(NK):
                    send_t[k, cq * 2 + h, s] = llm[48 * cq + 16 * k : 48 * cq + 16 * k + 16, lanes]

    pl.semaphore_wait(barrier, 15)

    def place(k, ys, yd, zl):
        off = (ys - yd + 4) % 4
        far = off // 2
        quarter = (1 - far) * (3 - off) + far * (off - 2)
        last = quarter // 3
        return last * (18 + 2 * k) + (1 - last) * (6 * k + 2 * quarter) + zl

    def t_send(k):
        for o in range(1, 8):
            send(
                send_t.at[k, (j + o) % 8], recv_t[k].at[pl.ds(j * 8, 8)],
                t_ss.at[k, o], t_rs.at[k, o], dev_t(o),
            )
        recv_t[k][pl.ds(j * 8, 8)] = send_t[k, j]

    def t_wait_d_send(k):
        for o in range(1, 8):
            await_recv(recv_t[k].at[pl.ds(((j + 8 - o) % 8) * 8, 8)], t_ss.at[k, o], t_rs.at[k, o], dev_t(o))

        @pl.loop(0, 64)
        def _(e):
            send_d[k, e // 8, e % 8] = recv_t[k][slot_ref[e]]

        for o in range(1, 8):
            qd = (q + o) % 8
            send(
                send_d.at[k, qd], own.at[j, place(k, y, qd // 2, zlo)],
                d_ss.at[k, o], d_rs.at[k, o], dev_q(o),
            )
        own[j, 18 + 2 * k + zlo] = send_d[k, q]

    def d_wait(k):
        for o in range(1, 8):
            qs = (q + 8 - o) % 8
            await_recv(
                own.at[j, place(k, qs // 2, y, qs % 2)], d_ss.at[k, o], d_rs.at[k, o], dev_q(o)
            )

    def piece(m, xx, zz):
        first, count = GROUPS[m]
        return own.at[2 * xx + zz, pl.ds(first, count)]

    def half(m, xx, zz, side):
        first, count = GROUPS[m]
        count //= 2
        return own.at[2 * xx + zz, pl.ds(first + side * count, count)]

    def g_send(m, n, ref, dev):
        send(ref, ref, g_ss.at[m, n], g_rs.at[m, n], dev)

    def g_wait(m, n, ref, dev):
        await_recv(ref, g_ss.at[m, n], g_rs.at[m, n], dev)

    oz = 1 - zhi

    def g_a(m):
        g_send(m, 0, piece(m, x, zhi), z2)
        g_send(m, 1, piece(m, x, zhi), dev_xr)
        g_send(m, 2, piece(m, x, zhi), dev_xl)

    def g_b(m):
        g_wait(m, 0, piece(m, x, oz), z2)
        g_send(m, 3, piece(m, x, oz), dev_xr)
        g_send(m, 4, piece(m, x, oz), dev_xl)

    def g_c(m):
        g_wait(m, 1, piece(m, xl, zhi), dev_xl)
        g_send(m, 5, half(m, xl, zhi, 0), dev_xr)
        g_wait(m, 2, piece(m, xr, zhi), dev_xr)
        g_send(m, 6, half(m, xr, zhi, 1), dev_xl)

    def g_e(m):
        g_wait(m, 3, piece(m, xl, oz), dev_xl)
        g_send(m, 7, half(m, xl, oz, 0), dev_xr)
        g_wait(m, 4, piece(m, xr, oz), dev_xr)
        g_send(m, 8, half(m, xr, oz, 1), dev_xl)

    def g_f(m):
        g_wait(m, 5, half(m, xo, zhi, 0), dev_xl)
        g_wait(m, 6, half(m, xo, zhi, 1), dev_xr)
        g_wait(m, 7, half(m, xo, oz, 0), dev_xl)
        g_wait(m, 8, half(m, xo, oz, 1), dev_xr)
        blocks = pl.ds(*GROUPS[m])
        send(
            own.at[:, blocks, pl.ds((1 - c) * 4, 4)], sib.at[:, blocks], s_ss.at[m], s_rs.at[m], sibling
        )

    def sib_wait(m):
        await_recv(sib.at[:, pl.ds(*GROUPS[m])], s_ss.at[m], s_rs.at[m], sibling)

    def hidden_rows(first, count):
        @pl.loop(first, first + count)
        def _(b):
            rows = pl.ds(pl.multiple_of(b * 32, 32), 32)
            value, slope_rows = gelu_parts(pre[rows, :].astype(F32))
            slope[rows, :] = slope_rows
            hid[pl.ds(pl.multiple_of(c * TOK + b * 32, 32), 32), :] = value.astype(BF)

    def down(first, count, store):
        @pl.loop(0, count)
        def _(qq):
            for cq in range(4):
                row = pl.ds(pl.multiple_of(qq * 64 + cq * 16, 16), 16)
                for img in range(8):
                    for h in range(2):
                        left[row, (img * 2 + h) * 128 : (img * 2 + h + 1) * 128] = own[
                            cq * 2 + h, first + qq, img
                        ]

        @pl.loop(0, 2)
        def _(n):
            cols = pl.ds(pl.multiple_of(n * 768, 768), 768)
            prod = jnp.dot(left[0 : count * 64, :], hid[:, cols], preferred_element_type=F32)
            prod = prod.reshape(count, 64, 768)
            for at in range(count):
                store(at, cols, prod[at])

    def down_a(k):
        def store(at, cols, rows):
            send_r[k, at, :, cols] = rows.astype(BF)

        down(6 * k, 2, store)
        for n in range(2):
            send(send_r.at[k, n], recv_a.at[k, n], a_ss.at[k, n], a_rs.at[k, n], dev_y(1 + 2 * n))

    def r_send(k, at):
        n, zz = at // 2, at % 2
        send(
            send_r.at[k, 2 + at], recv_r.at[k, n, zz], r_ss.at[k, at], r_rs.at[k, at], dev_y(TO_Y[n])
        )

    def down_b(k):
        def store(at, cols, rows):
            if at in (1, 2):
                wait_r[at - 1, :, cols] = rows
            else:
                send_r[k, 2 + at, :, cols] = rows.astype(BF)

        down(6 * k + 2, 4, store)
        r_send(k, 0)
        r_send(k, 3)

    def relay(k):
        for n in range(2):
            await_recv(recv_a.at[k, n], a_ss.at[k, n], a_rs.at[k, n], dev_y(3 - 2 * n))

        @pl.loop(0, 4)
        def _(b):
            rows = pl.ds(pl.multiple_of(b * 16, 16), 16)
            for n in range(2):
                total = wait_r[n, rows, :] + recv_a[k, 1 - n, rows, :].astype(F32)
                send_r[k, 3 + n, rows, :] = total.astype(BF)

        r_send(k, 1)
        r_send(k, 2)

    def down_c(k, chunks):
        def store(at, cols, rows):
            mine[k + at // 2, at % 2, :, cols] = rows

        down(18 + 2 * k, 2 * chunks, store)

    def r_sum(k):
        for at in range(4):
            n, zz = at // 2, at % 2
            await_recv(recv_r.at[k, n, zz], r_ss.at[k, at], r_rs.at[k, at], dev_y(TO_Y[1 - n]))

        @pl.loop(0, 4)
        def _(b):
            rows = pl.ds(pl.multiple_of(b * 16, 16), 16)
            for side in range(2):
                zz = zlo if side == 0 else 1 - zlo
                total = mine[k, zz, rows, :]
                for o in range(2):
                    total += recv_r[k, o, zz, rows, :].astype(F32)
                if side == 0:
                    mine[k, zz, rows, :] = total
                else:
                    send_z[k, rows, :] = total.astype(BF)

        send(send_z.at[k], recv_z.at[k], z_ss.at[k], z_rs.at[k], zpart)

    def r_final(k):
        await_recv(recv_z.at[k], z_ss.at[k], z_rs.at[k], zpart)

        @pl.loop(0, 4)
        def _(cq):
            rows = pl.ds(pl.multiple_of(cq * 16, 16), 16)
            total = mine[k, zlo, rows, :] + recv_z[k, rows, :].astype(F32)
            fin[pl.ds(pl.multiple_of(cq * 48 + k * 16, 16), 16), :] = total * (1.0 / 128.0)

    def order_w(b):
        rows = pl.ds(b * 512, 512)
        out = lax.broadcasted_iota(jnp.int32, (384, 384), 1)
        source = ((out >> 6) & 1) * 192 + ((out >> 4) & 3) * 48 + (out >> 7) * 16 + (out & 15)
        perm = (lax.broadcasted_iota(jnp.int32, (384, 384), 0) == source).astype(F32).astype(BF)

        @pl.loop(0, 8)
        def _(u):
            cols = pl.ds(pl.multiple_of(u * 384, 384), 384)
            w[rows, cols] = jnp.dot(w[rows, cols], perm, preferred_element_type=F32).astype(BF)

    def up(g, b):
        first, count = GROUPS[g]

        def source(at):
            if g < 3:
                return g, 2 * ((y + (2, 3, 1)[at // 2]) % 4) + at % 2
            return 2 * (g - 3) + at // 2, 2 * y + at % 2

        for at in range(count):
            for cq in range(4):
                for n in range(4):
                    lanes = slice(n * 128, (n + 1) * 128)
                    img, h = 2 * b + n // 2, n % 2
                    for p, rows in (
                        (c, own[cq * 2 + h, first + at, c * 4 + img]),
                        (1 - c, sib[cq * 2 + h, first + at, img]),
                    ):
                        row = pl.multiple_of(at * 128 + p * 64 + cq * 16, 16)
                        rhs[pl.ds(row, 16), lanes] = rows

        tokens = slice(b * 512, (b + 1) * 512)

        @pl.loop(0, 2)
        def _(n):
            fs = pl.ds(pl.multiple_of(n * 768, 768), 768)
            blocks = []
            for at in range(count):
                k, qq = source(at)
                blocks.append(w[fs, pl.ds(pl.multiple_of(qq * 384 + k * 128, 128), 128)])
            lhs = jnp.concatenate(blocks, axis=1)
            part = jnp.dot(lhs, rhs[0 : count * 128, :], preferred_element_type=F32)
            if g > 0:
                part += ghacc[fs, tokens]
            if g < 4:
                ghacc[fs, tokens] = part
            else:
                pre[tokens, fs] = (part.T * slope[tokens, fs]).astype(BF)


    t_send(0)
    cp_pre.wait()
    hidden_rows(0, 16)
    t_wait_d_send(0)
    t_send(1)
    t_send(2)
    cp_w.wait()
    order_w(0)
    d_wait(0)
    g_a(0)
    t_wait_d_send(1)
    hidden_rows(16, 4)
    g_b(0)
    t_wait_d_send(2)
    hidden_rows(20, 6)
    g_c(0)
    hidden_rows(26, 6)
    send(hid.at[pl.ds(c * TOK, TOK)], hid.at[pl.ds(c * TOK, TOK)], h_ss.at[0], h_rs.at[0], sibling)
    g_e(0)
    d_wait(1)
    g_a(1)
    order_w(1)
    g_b(1)
    g_f(0)
    await_recv(hid.at[pl.ds((1 - c) * TOK, TOK)], h_ss.at[0], h_rs.at[0], sibling)
    down_a(0)
    g_c(1)
    d_wait(2)
    g_a(2)
    down_b(0)
    order_w(2)
    g_e(1)
    g_b(2)
    relay(0)
    sib_wait(0)
    up(0, 0)
    g_f(1)
    down_a(1)
    g_c(2)
    g_a(3)
    down_b(1)
    up(0, 1)
    g_e(2)
    g_b(3)
    relay(1)
    sib_wait(1)
    up(1, 0)
    up(1, 1)
    g_f(2)
    down_a(2)
    g_c(3)
    g_a(4)
    down_b(2)
    g_e(3)
    g_b(4)
    g_c(4)
    relay(2)
    sib_wait(2)
    up(2, 0)
    g_f(3)
    g_e(4)
    down_c(0, 2)
    r_sum(0)
    r_sum(1)
    sib_wait(3)
    up(2, 1)
    up(3, 0)
    up(3, 1)
    g_f(4)
    down_c(2, 1)
    r_sum(2)
    r_final(0)
    r_final(1)
    sib_wait(4)
    up(4, 0)
    up(4, 1)
    r_final(2)
    for cp in sends:
        cp.wait_send()


def on_device(llm_grad, image_slot, pre_act, w_down):
    dma = pltpu.SemaphoreType.DMA
    any_space = pl.BlockSpec(memory_space=pl.ANY)
    grad_pre, down = pl.pallas_call(
        kernel,
        out_shape=(
            pltpu.VMEM((TOK, NF), BF),
            pltpu.VMEM((192, NF), F32),
        ),
        in_specs=[pl.BlockSpec(memory_space=pltpu.SMEM), any_space, any_space, any_space],
        out_specs=(pl.BlockSpec(memory_space=pltpu.VMEM), pl.BlockSpec(memory_space=pltpu.VMEM)),
        scratch_shapes=[
            pltpu.VMEM((192, 2048), BF),
            pltpu.VMEM((NF, 3072), BF),
            pltpu.VMEM((NK, 8, 8, 16, 128), BF),
            pltpu.VMEM((64, 16, 128), BF),
            pltpu.VMEM((64, 16, 128), BF),
            pltpu.VMEM((64, 16, 128), BF),
            pltpu.VMEM((NK, 8, 8, 16, 128), BF),
            pltpu.VMEM((8, 24, 8, 16, 128), BF),
            pltpu.VMEM((8, 24, 4, 16, 128), BF),
            pltpu.VMEM((2 * TOK, NF), BF),
            pltpu.VMEM((256, 2048), BF),
            pltpu.VMEM((NF, TOK), F32),
            pltpu.VMEM((NK, 6, 64, NF), BF),
            pltpu.VMEM((2, 64, NF), F32),
            pltpu.VMEM((NK, 2, 64, NF), BF),
            pltpu.VMEM((NK, 2, 2, 64, NF), BF),
            pltpu.VMEM((NK, 2, 64, NF), F32),
            pltpu.VMEM((NK, 64, NF), BF),
            pltpu.VMEM((NK, 64, NF), BF),
            pltpu.VMEM((768, 512), BF),
            pltpu.VMEM((TOK, NF), F32),
            dma((3,)), dma((1,)),
            dma((NK, 8)), dma((NK, 8)), dma((NK, 8)), dma((NK, 8)),
            dma((5, 9)), dma((5, 9)), dma((5,)), dma((5,)), dma((1,)), dma((1,)),
            dma((NK, 2)), dma((NK, 2)), dma((NK, 4)), dma((NK, 4)), dma((NK,)), dma((NK,)),
        ],
        compiler_params=pltpu.CompilerParams(
            collective_id=0, has_side_effects=True, vmem_limit_bytes=56 << 20
        ),
        cost_estimate=pl.CostEstimate(
            flops=19_327_352_832, bytes_accessed=18 << 20, transcendentals=3_000_000
        ),
    )(image_slot, llm_grad.T, pre_act, w_down)
    return (grad_pre, down.T)


def solution(mesh):
    placed = (P("tensor", "dp"), P(), P("dp", "tensor"), P("tensor", None))
    return jax.shard_map(
        on_device,
        mesh=mesh,
        in_specs=placed,
        out_specs=(P("dp", "tensor"), P("tensor", "dp")),
        check_vma=False,
    )
```

```python
import jax
import jax.numpy as jnp
from jax import lax
from jax.experimental import pallas as pl
from jax.experimental.pallas import tpu as pltpu
from jax.sharding import PartitionSpec as P

MESH = pl.DeviceIdType.MESH
BF = jnp.bfloat16
F32 = jnp.float32
NK = 3
TOK = 1024
NF = 1536
GROUPS = ((0, 6), (6, 6), (12, 6), (18, 4), (22, 2))
TO_Y = (3, 1)


def gelu_parts(value):
    inner = 0.7978845608 * (value + 0.044715 * value * value * value)
    tanh_value = jnp.tanh(inner)
    out = 0.5 * value * (1.0 + tanh_value)
    slope = 0.5 * (1.0 + tanh_value) + 0.5 * value * (
        1.0 - tanh_value * tanh_value
    ) * 0.7978845608 * (1.0 + 3.0 * 0.044715 * value * value)
    return (out, slope)


def kernel(
    slot_ref, llm_hbm, pre_hbm, w_hbm, pre, fin,
    llm, w, send_t, recv_t0, recv_t1, recv_t2, send_d, own, sib, hid,
    left, ghacc, send_r, wait_r, recv_a, recv_r, mine, send_z, recv_z, rhs, slope,
    in_sem, out_sem, t_ss, t_rs, d_ss, d_rs, g_ss, g_rs, s_ss, s_rs, h_ss, h_rs,
    a_ss, a_rs, r_ss, r_rs, z_ss, z_rs,
):
    recv_t = (recv_t0, recv_t1, recv_t2)
    dp = lax.axis_index("dp")
    j = lax.axis_index("tensor")
    y, zlo, c = dp // 4, (dp // 2) % 2, dp % 2
    x, zhi = j // 2, j % 2
    q = dp // 2

    def dev_t(o):
        return (dp, (j + o) % 8)

    def dev_q(o):
        return (((q + o) % 8) * 2 + c, j)

    sibling = (dp - c + (1 - c), j)
    z2 = (dp, 2 * x + (1 - zhi))
    xr, xl, xo = (x + 1) % 4, (x + 3) % 4, (x + 2) % 4
    dev_xr, dev_xl = (dp, 2 * xr + zhi), (dp, 2 * xl + zhi)
    zpart = ((y * 2 + (1 - zlo)) * 2 + c, j)

    def dev_y(o):
        return ((((y + o) % 4) * 2 + zlo) * 2 + c, j)

    def rcopy(src, dst, ss, rs, dev):
        return pltpu.make_async_remote_copy(
            src_ref=src, dst_ref=dst, send_sem=ss, recv_sem=rs, device_id=dev, device_id_type=MESH
        )

    sends = []

    def send(src, dst, ss, rs, dev):
        cp = rcopy(src, dst, ss, rs, dev)
        cp.start()
        sends.append(cp)

    def await_recv(land, ss, rs, dev):
        rcopy(land, land, ss, rs, dev).wait_recv()

    cp_llm = pltpu.make_async_copy(llm_hbm, llm, in_sem.at[0])
    cp_pre = pltpu.make_async_copy(pre_hbm, pre, in_sem.at[1])
    cp_w = pltpu.make_async_copy(w_hbm, w, in_sem.at[2])
    cp_llm.start()
    cp_pre.start()
    cp_w.start()
    barrier = pltpu.get_barrier_semaphore()
    for o in range(1, 8):
        pl.semaphore_signal(barrier, inc=1, device_id=dev_t(o), device_id_type=MESH)
        pl.semaphore_signal(barrier, inc=1, device_id=dev_q(o), device_id_type=MESH)
    pl.semaphore_signal(barrier, inc=1, device_id=sibling, device_id_type=MESH)
    cp_llm.wait()

    @pl.loop(0, 8)
    def _(s):
        for h in range(2):
            lanes = pl.ds(pl.multiple_of(s * 256 + h * 128, 128), 128)
            for cq in range(4):
                for k in range(NK):
                    send_t[k, cq * 2 + h, s] = llm[48 * cq + 16 * k : 48 * cq + 16 * k + 16, lanes]

    pl.semaphore_wait(barrier, 15)

    def place(k, ys, yd, zl):
        off = (ys - yd + 4) % 4
        far = off // 2
        quarter = (1 - far) * (3 - off) + far * (off - 2)
        last = quarter // 3
        return last * (18 + 2 * k) + (1 - last) * (6 * k + 2 * quarter) + zl

    def t_send(k):
        for o in range(1, 8):
            send(
                send_t.at[k, (j + o) % 8], recv_t[k].at[pl.ds(j * 8, 8)],
                t_ss.at[k, o], t_rs.at[k, o], dev_t(o),
            )
        recv_t[k][pl.ds(j * 8, 8)] = send_t[k, j]

    def t_wait_d_send(k):
        for o in range(1, 8):
            await_recv(recv_t[k].at[pl.ds(((j + 8 - o) % 8) * 8, 8)], t_ss.at[k, o], t_rs.at[k, o], dev_t(o))

        @pl.loop(0, 64)
        def _(e):
            send_d[k, e // 8, e % 8] = recv_t[k][slot_ref[e]]

        for o in range(1, 8):
            qd = (q + o) % 8
            send(
                send_d.at[k, qd], own.at[j, place(k, y, qd // 2, zlo)],
                d_ss.at[k, o], d_rs.at[k, o], dev_q(o),
            )
        own[j, 18 + 2 * k + zlo] = send_d[k, q]

    def d_wait(k):
        for o in range(1, 8):
            qs = (q + 8 - o) % 8
            await_recv(
                own.at[j, place(k, qs // 2, y, qs % 2)], d_ss.at[k, o], d_rs.at[k, o], dev_q(o)
            )

    def piece(m, xx, zz):
        first, count = GROUPS[m]
        return own.at[2 * xx + zz, pl.ds(first, count)]

    def half(m, xx, zz, side):
        first, count = GROUPS[m]
        count //= 2
        return own.at[2 * xx + zz, pl.ds(first + side * count, count)]

    def g_send(m, n, ref, dev):
        send(ref, ref, g_ss.at[m, n], g_rs.at[m, n], dev)

    def g_wait(m, n, ref, dev):
        await_recv(ref, g_ss.at[m, n], g_rs.at[m, n], dev)

    oz = 1 - zhi

    def g_a(m):
        g_send(m, 0, piece(m, x, zhi), z2)
        g_send(m, 1, piece(m, x, zhi), dev_xr)
        g_send(m, 2, piece(m, x, zhi), dev_xl)

    def g_b(m):
        g_wait(m, 0, piece(m, x, oz), z2)
        g_send(m, 3, piece(m, x, oz), dev_xr)
        g_send(m, 4, piece(m, x, oz), dev_xl)

    def g_c(m):
        g_wait(m, 1, piece(m, xl, zhi), dev_xl)
        g_send(m, 5, half(m, xl, zhi, 0), dev_xr)
        g_wait(m, 2, piece(m, xr, zhi), dev_xr)
        g_send(m, 6, half(m, xr, zhi, 1), dev_xl)

    def g_e(m):
        g_wait(m, 3, piece(m, xl, oz), dev_xl)
        g_send(m, 7, half(m, xl, oz, 0), dev_xr)
        g_wait(m, 4, piece(m, xr, oz), dev_xr)
        g_send(m, 8, half(m, xr, oz, 1), dev_xl)

    def g_f(m):
        g_wait(m, 5, half(m, xo, zhi, 0), dev_xl)
        g_wait(m, 6, half(m, xo, zhi, 1), dev_xr)
        g_wait(m, 7, half(m, xo, oz, 0), dev_xl)
        g_wait(m, 8, half(m, xo, oz, 1), dev_xr)
        blocks = pl.ds(*GROUPS[m])
        send(
            own.at[:, blocks, pl.ds((1 - c) * 4, 4)], sib.at[:, blocks], s_ss.at[m], s_rs.at[m], sibling
        )

    def sib_wait(m):
        await_recv(sib.at[:, pl.ds(*GROUPS[m])], s_ss.at[m], s_rs.at[m], sibling)

    def hidden_rows(first, count):
        @pl.loop(first, first + count)
        def _(b):
            rows = pl.ds(pl.multiple_of(b * 32, 32), 32)
            value, slope_rows = gelu_parts(pre[rows, :].astype(F32))
            slope[rows, :] = slope_rows
            hid[pl.ds(pl.multiple_of(c * TOK + b * 32, 32), 32), :] = value.astype(BF)

    def down(first, count, store):
        @pl.loop(0, count)
        def _(qq):
            for cq in range(4):
                row = pl.ds(pl.multiple_of(qq * 64 + cq * 16, 16), 16)
                for img in range(8):
                    for h in range(2):
                        left[row, (img * 2 + h) * 128 : (img * 2 + h + 1) * 128] = own[
                            cq * 2 + h, first + qq, img
                        ]

        @pl.loop(0, 2)
        def _(n):
            cols = pl.ds(pl.multiple_of(n * 768, 768), 768)
            prod = jnp.dot(left[0 : count * 64, :], hid[:, cols], preferred_element_type=F32)
            prod = prod.reshape(count, 64, 768)
            for at in range(count):
                store(at, cols, prod[at])

    def down_a(k):
        def store(at, cols, rows):
            send_r[k, at, :, cols] = rows.astype(BF)

        down(6 * k, 2, store)
        for n in range(2):
            send(send_r.at[k, n], recv_a.at[k, n], a_ss.at[k, n], a_rs.at[k, n], dev_y(1 + 2 * n))

    def r_send(k, at):
        n, zz = at // 2, at % 2
        send(
            send_r.at[k, 2 + at], recv_r.at[k, n, zz], r_ss.at[k, at], r_rs.at[k, at], dev_y(TO_Y[n])
        )

    def down_b(k):
        def store(at, cols, rows):
            if at in (1, 2):
                wait_r[at - 1, :, cols] = rows
            else:
                send_r[k, 2 + at, :, cols] = rows.astype(BF)

        down(6 * k + 2, 4, store)
        r_send(k, 0)
        r_send(k, 3)

    def relay(k):
        for n in range(2):
            await_recv(recv_a.at[k, n], a_ss.at[k, n], a_rs.at[k, n], dev_y(3 - 2 * n))

        @pl.loop(0, 4)
        def _(b):
            rows = pl.ds(pl.multiple_of(b * 16, 16), 16)
            for n in range(2):
                total = wait_r[n, rows, :] + recv_a[k, 1 - n, rows, :].astype(F32)
                send_r[k, 3 + n, rows, :] = total.astype(BF)

        r_send(k, 1)
        r_send(k, 2)

    def down_c(k, chunks):
        def store(at, cols, rows):
            mine[k + at // 2, at % 2, :, cols] = rows

        down(18 + 2 * k, 2 * chunks, store)

    def r_sum(k):
        for at in range(4):
            n, zz = at // 2, at % 2
            await_recv(recv_r.at[k, n, zz], r_ss.at[k, at], r_rs.at[k, at], dev_y(TO_Y[1 - n]))

        @pl.loop(0, 4)
        def _(b):
            rows = pl.ds(pl.multiple_of(b * 16, 16), 16)
            for side in range(2):
                zz = zlo if side == 0 else 1 - zlo
                total = mine[k, zz, rows, :]
                for o in range(2):
                    total += recv_r[k, o, zz, rows, :].astype(F32)
                if side == 0:
                    mine[k, zz, rows, :] = total
                else:
                    send_z[k, rows, :] = total.astype(BF)

        send(send_z.at[k], recv_z.at[k], z_ss.at[k], z_rs.at[k], zpart)

    def r_final(k):
        await_recv(recv_z.at[k], z_ss.at[k], z_rs.at[k], zpart)

        @pl.loop(0, 4)
        def _(cq):
            rows = pl.ds(pl.multiple_of(cq * 16, 16), 16)
            total = mine[k, zlo, rows, :] + recv_z[k, rows, :].astype(F32)
            fin[pl.ds(pl.multiple_of(cq * 48 + k * 16, 16), 16), :] = total * (1.0 / 128.0)

    def order_w(b):
        rows = pl.ds(b * 512, 512)
        out = lax.broadcasted_iota(jnp.int32, (384, 384), 1)
        source = ((out >> 6) & 1) * 192 + ((out >> 4) & 3) * 48 + (out >> 7) * 16 + (out & 15)
        perm = (lax.broadcasted_iota(jnp.int32, (384, 384), 0) == source).astype(F32).astype(BF)

        @pl.loop(0, 8)
        def _(u):
            cols = pl.ds(pl.multiple_of(u * 384, 384), 384)
            w[rows, cols] = jnp.dot(w[rows, cols], perm, preferred_element_type=F32).astype(BF)

    def up(g, b):
        first, count = GROUPS[g]

        def source(at):
            if g < 3:
                return g, 2 * ((y + (2, 3, 1)[at // 2]) % 4) + at % 2
            return 2 * (g - 3) + at // 2, 2 * y + at % 2

        for at in range(count):
            for cq in range(4):
                for n in range(4):
                    lanes = slice(n * 128, (n + 1) * 128)
                    img, h = 2 * b + n // 2, n % 2
                    for p, rows in (
                        (c, own[cq * 2 + h, first + at, c * 4 + img]),
                        (1 - c, sib[cq * 2 + h, first + at, img]),
                    ):
                        row = pl.multiple_of(at * 128 + p * 64 + cq * 16, 16)
                        rhs[pl.ds(row, 16), lanes] = rows

        tokens = slice(b * 512, (b + 1) * 512)

        @pl.loop(0, 2)
        def _(n):
            fs = pl.ds(pl.multiple_of(n * 768, 768), 768)
            blocks = []
            for at in range(count):
                k, qq = source(at)
                blocks.append(w[fs, pl.ds(pl.multiple_of(qq * 384 + k * 128, 128), 128)])
            lhs = jnp.concatenate(blocks, axis=1)
            part = jnp.dot(lhs, rhs[0 : count * 128, :], preferred_element_type=F32)
            if g > 0:
                part += ghacc[fs, tokens]
            if g < 4:
                ghacc[fs, tokens] = part
            else:
                pre[tokens, fs] = (part.T * slope[tokens, fs]).astype(BF)


    t_send(0)
    cp_pre.wait()
    hidden_rows(0, 16)
    t_wait_d_send(0)
    t_send(1)
    t_send(2)
    cp_w.wait()
    order_w(0)
    d_wait(0)
    g_a(0)
    t_wait_d_send(1)
    hidden_rows(16, 4)
    g_b(0)
    t_wait_d_send(2)
    hidden_rows(20, 6)
    g_c(0)
    hidden_rows(26, 6)
    send(hid.at[pl.ds(c * TOK, TOK)], hid.at[pl.ds(c * TOK, TOK)], h_ss.at[0], h_rs.at[0], sibling)
    g_e(0)
    d_wait(1)
    g_a(1)
    order_w(1)
    g_b(1)
    g_f(0)
    await_recv(hid.at[pl.ds((1 - c) * TOK, TOK)], h_ss.at[0], h_rs.at[0], sibling)
    down_a(0)
    g_c(1)
    d_wait(2)
    g_a(2)
    down_b(0)
    order_w(2)
    g_e(1)
    g_b(2)
    relay(0)
    sib_wait(0)
    up(0, 0)
    g_f(1)
    down_a(1)
    g_c(2)
    g_a(3)
    down_b(1)
    up(0, 1)
    g_e(2)
    g_b(3)
    relay(1)
    sib_wait(1)
    up(1, 0)
    up(1, 1)
    g_f(2)
    down_a(2)
    g_c(3)
    g_a(4)
    down_b(2)
    g_e(3)
    g_b(4)
    g_c(4)
    relay(2)
    sib_wait(2)
    up(2, 0)
    g_f(3)
    g_e(4)
    down_c(0, 2)
    r_sum(0)
    r_sum(1)
    sib_wait(3)
    up(2, 1)
    up(3, 0)
    up(3, 1)
    r_final(0)
    g_f(4)
    down_c(2, 1)
    r_final(1)
    r_sum(2)
    sib_wait(4)
    up(4, 0)
    up(4, 1)
    r_final(2)
    for cp in sends:
        cp.wait_send()


def on_device(llm_grad, image_slot, pre_act, w_down):
    dma = pltpu.SemaphoreType.DMA
    any_space = pl.BlockSpec(memory_space=pl.ANY)
    grad_pre, down = pl.pallas_call(
        kernel,
        out_shape=(
            pltpu.VMEM((TOK, NF), BF),
            pltpu.VMEM((192, NF), F32),
        ),
        in_specs=[pl.BlockSpec(memory_space=pltpu.SMEM), any_space, any_space, any_space],
        out_specs=(pl.BlockSpec(memory_space=pltpu.VMEM), pl.BlockSpec(memory_space=pltpu.VMEM)),
        scratch_shapes=[
            pltpu.VMEM((192, 2048), BF),
            pltpu.VMEM((NF, 3072), BF),
            pltpu.VMEM((NK, 8, 8, 16, 128), BF),
            pltpu.VMEM((64, 16, 128), BF),
            pltpu.VMEM((64, 16, 128), BF),
            pltpu.VMEM((64, 16, 128), BF),
            pltpu.VMEM((NK, 8, 8, 16, 128), BF),
            pltpu.VMEM((8, 24, 8, 16, 128), BF),
            pltpu.VMEM((8, 24, 4, 16, 128), BF),
            pltpu.VMEM((2 * TOK, NF), BF),
            pltpu.VMEM((256, 2048), BF),
            pltpu.VMEM((NF, TOK), F32),
            pltpu.VMEM((NK, 6, 64, NF), BF),
            pltpu.VMEM((2, 64, NF), F32),
            pltpu.VMEM((NK, 2, 64, NF), BF),
            pltpu.VMEM((NK, 2, 2, 64, NF), BF),
            pltpu.VMEM((NK, 2, 64, NF), F32),
            pltpu.VMEM((NK, 64, NF), BF),
            pltpu.VMEM((NK, 64, NF), BF),
            pltpu.VMEM((768, 512), BF),
            pltpu.VMEM((TOK, NF), F32),
            dma((3,)), dma((1,)),
            dma((NK, 8)), dma((NK, 8)), dma((NK, 8)), dma((NK, 8)),
            dma((5, 9)), dma((5, 9)), dma((5,)), dma((5,)), dma((1,)), dma((1,)),
            dma((NK, 2)), dma((NK, 2)), dma((NK, 4)), dma((NK, 4)), dma((NK,)), dma((NK,)),
        ],
        compiler_params=pltpu.CompilerParams(
            collective_id=0, has_side_effects=True, vmem_limit_bytes=56 << 20
        ),
        cost_estimate=pl.CostEstimate(
            flops=19_327_352_832, bytes_accessed=18 << 20, transcendentals=3_000_000
        ),
    )(image_slot, llm_grad.T, pre_act, w_down)
    return (grad_pre, down.T)


def solution(mesh):
    placed = (P("tensor", "dp"), P(), P("dp", "tensor"), P("tensor", None))
    return jax.shard_map(
        on_device,
        mesh=mesh,
        in_specs=placed,
        out_specs=(P("dp", "tensor"), P("tensor", "dp")),
        check_vma=False,
    )
```
